32 devices in a mesh: row: 4 (over x, core), col: 8 (over z, y).
Axes of the slice: x: 2, y: 2, z: 4, core: 2. Of those that a mesh axis runs over, the one named last changes fastest.
Arguments:
- basis: bfloat16 [8192, 256], P(('row', 'col')), may hold values from -6 to 6
- degree_scale: float32 [8192], P(('row', 'col')), may hold values from 0.5 to 3
- tile_data: bfloat16 [64, 8, 8, 128, 128], P('row', 'col'), may hold values from -0.125 to 0.125
- tile_index: int32 [64, 8, 8], P('row', 'col'), may hold values from 0 to 7, as said below
- tile_count: int32 [64, 8], P('row', 'col'), may hold values from 1 to 8, as said below
Outputs:
- embedding: float32 [8192, 256], P(('row', 'col'))
- factor: float32 [256, 256], replicated
The draws below stay inside these ranges and needn't reach their ends.
Inputs may be any that keep to these rules, and one draw needn't show every extreme that they name: `tile_index`: all 8 entries of one tile row in one column block are distinct. `tile_count`: some tile row has 8 live slots in every draw; loads differ widely between devices.
All inputs are finite; a program needn't handle non-finite values.
Results may differ from the reference program's by a relative error of at most 0.034.
Values may be sent and summed in bfloat16 or wider, within the bound.
A program may use at most 128 MiB of HBM per device.

```python
import math
import jax
import jax.numpy as jnp
from jax import lax

K = 256
TILE = 128
SLOTS = 8
ROW_TILES_DEV = 2
ITERS = 4
ROWS_DEV = 256
NODES = 8192
TROWS = 64
TCOLS = 8
N_ROW = 4
N_COL = 8


def draw_degree_scale(key, part):
    position = jnp.arange(NODES, dtype=jnp.float32) / NODES
    spread = jax.random.uniform(key, (NODES,), jnp.float32, math.log(0.7), math.log(1.4))
    rise = position * math.log(1.8)
    return jnp.exp(spread + rise)


def draw_tile_index(key, part):
    scores = jax.random.randint(key, (TROWS, N_COL, TCOLS), 0, 1 << 20) * TCOLS + jnp.arange(TCOLS)
    order = jnp.argsort(scores, axis=-1)
    return order[..., :SLOTS].astype(jnp.int32)


def draw_tile_count(key, part):
    keys = jax.random.split(key, 5)
    row_tiles = N_COL * ROW_TILES_DEV
    first = jax.random.randint(keys[0], (N_ROW, 1, N_COL), 1, SLOTS + 1)
    second = jax.random.randint(keys[1], (N_ROW, 1, N_COL), 1, SLOTS + 1)
    level = jnp.maximum(first * second // SLOTS, 1)
    busy = jax.random.randint(keys[2], (), 0, N_ROW * N_COL)
    device_ids = jnp.arange(N_ROW * N_COL).reshape(N_ROW, 1, N_COL)
    level = jnp.where(device_ids == busy, SLOTS, level)
    counts = jax.random.randint(keys[3], (N_ROW, row_tiles, N_COL), (level + 1) // 2, level + 1)
    fullest = jax.random.randint(keys[4], (N_ROW, 1, N_COL), 0, row_tiles)
    counts = jnp.where(jnp.arange(row_tiles)[None, :, None] == fullest, level, counts)
    return counts.reshape(TROWS, N_COL).astype(jnp.int32)


def level_of(key, dims, pieces, low, high):
    def one(dim, blocks):
        draws = jax.random.uniform(jax.random.fold_in(jax.random.fold_in(key, 6), dim), (blocks,), jnp.float32, low / len(pieces), high / len(pieces))
        return jnp.repeat(jnp.exp(draws), dims[dim] // blocks).reshape((-1,) + (1,) * (len(dims) - dim - 1))

    factor_of = one(*pieces[0])
    for cut in pieces[1:]:
        factor_of = factor_of * one(*cut)
    return factor_of


def noise(key, extent, width, bound, cuts=(), kind=jnp.bfloat16):
    level = level_of(key, extent, cuts, -0.22, 0.18) if cuts else 1.0
    result = jax.random.normal(key, extent, jnp.float32) * width * level
    return jnp.minimum(jnp.maximum(result, -bound), bound).astype(kind)


def setup_inputs(seed: int = 0) -> dict:
    arg_keys = jax.random.split(jax.random.key(seed), 6)
    basis = noise(arg_keys[0], (NODES, K), 1.0, 6.0, ((0, 32),))
    degree_scale = draw_degree_scale(jax.random.fold_in(arg_keys[5], 71), 0)
    tile_data = noise(arg_keys[2], (TROWS, N_COL, SLOTS, TILE, TILE), (N_COL * SLOTS * TILE // 4) ** -0.5, 0.125, ((0, 4), (1, 8)))
    tile_index = draw_tile_index(jax.random.fold_in(arg_keys[5], 71), 0)
    tile_count = draw_tile_count(jax.random.fold_in(arg_keys[5], 71), 0)
    return dict(basis=basis, degree_scale=degree_scale, tile_data=tile_data, tile_index=tile_index, tile_count=tile_count)


def apply_operator(probe, tile_data, tile_index, tile_count):
    blocks = probe.reshape(N_ROW, N_COL, ROWS_DEV, K).transpose(1, 0, 2, 3).reshape(N_COL, TCOLS, TILE, K)
    slot_ids = jnp.arange(SLOTS)
    col_ids = jnp.arange(N_COL)

    def one_row(packed):
        tiles, chosen_index, live_count = packed
        chosen = blocks[col_ids[:, None], chosen_index]
        alive = slot_ids[None, :] < live_count[:, None]
        chosen = jnp.where(alive[:, :, None, None], chosen.astype(jnp.float32), jnp.float32(0.0))
        term = jnp.einsum('jsab,jsbk->jak', tiles.astype(jnp.float32), chosen)
        term = lax.optimization_barrier(term.astype(jnp.bfloat16)).astype(jnp.float32)
        return jnp.sum(term, axis=0)
    rows = lax.map(one_row, (tile_data, tile_index, tile_count))
    return rows.reshape(NODES, K)

def reference(basis, degree_scale, tile_data, tile_index, tile_count):
    scale = degree_scale[:, None]
    probe = (basis.astype(jnp.float32) * scale).astype(jnp.bfloat16)
    embedding = None
    factor = None
    for step in range(ITERS):
        image = apply_operator(probe, tile_data, tile_index, tile_count) * scale
        gram = lax.dot_general(image, image, (((0,), (0,)), ((), ())), precision=lax.Precision.HIGHEST) / NODES
        lower = jnp.linalg.cholesky(gram)
        embedding = jax.scipy.linalg.solve_triangular(lower, image.T, lower=True).T
        factor = lower.T
        probe = (embedding * scale).astype(jnp.bfloat16)
    return (embedding, factor)
```

```python
import functools

import jax
import jax.numpy as jnp
from jax import lax
from jax.experimental import pallas as pl
from jax.experimental.pallas import tpu as pltpu
from jax.sharding import PartitionSpec as P

ITERS = 4
LEAF = 128
STEP = 8
F32 = jnp.float32
BF16 = jnp.bfloat16
EXACT = lax.Precision.HIGHEST
MESH = pl.DeviceIdType.MESH
VMEM_BYTES = 56 * 1024 * 1024


def densify_kernel(index_ref, count_ref, tiles_ref, out_ref):
    row = pl.program_id(0)
    slots, tile = tiles_ref.shape[1], tiles_ref.shape[2]
    out_ref[...] = jnp.zeros_like(out_ref)
    for slot in range(slots):

        @pl.when(slot < count_ref[row])
        def _():
            column = pl.multiple_of(index_ref[row, slot] * tile, tile)
            out_ref[:, pl.ds(column, tile)] = tiles_ref[0, slot]


def densify(tiles, index, counts, columns):
    rows, slots, tile, _ = tiles.shape
    return pl.pallas_call(
        densify_kernel,
        grid_spec=pltpu.PrefetchScalarGridSpec(
            num_scalar_prefetch=2,
            grid=(rows,),
            in_specs=[pl.BlockSpec((1, slots, tile, tile), lambda i, *_: (i, 0, 0, 0))],
            out_specs=pl.BlockSpec((tile, columns), lambda i, *_: (i, 0)),
        ),
        out_shape=jax.ShapeDtypeStruct((rows * tile, columns), BF16),
    )(index, counts, tiles)


def leaf_factor(gram):
    size = gram.shape[0]
    rows = lax.broadcasted_iota(jnp.int32, (size, size), 0)
    lanes = lax.broadcasted_iota(jnp.int32, (size, size), 1)
    eye = (rows == lanes).astype(F32)

    def group(g, state):
        work, left = state
        for j in range(STEP):
            pivot_row = work[j : j + 1, :]
            left_row = left[j : j + 1, :]
            column = jnp.broadcast_to(work[:, j : j + 1], (size, size))
            pivot = column[j : j + 1, :]
            open_rows = (rows > j) & (rows < size - STEP * g)
            ratio = jnp.where(open_rows, column * (1.0 / pivot), 0.0)
            work = work - ratio * pivot_row
            left = left - ratio * left_row
        work = jnp.concatenate([work[STEP:], work[:STEP]], axis=0)
        left = jnp.concatenate([left[STEP:], left[:STEP]], axis=0)
        work = pltpu.roll(work, size - STEP, 1)
        return work, left

    work, left = lax.fori_loop(0, size // STEP, group, (gram, eye))
    diagonal = jnp.sum(work * eye, axis=1, keepdims=True)
    inverse = lax.rsqrt(diagonal)
    upper = jnp.where(rows <= lanes, work * inverse, 0.0)
    return upper, left * inverse


def exact_dot(a, b, dims=((1,), (0,))):
    return lax.dot_general(a, b, (dims, ((), ())), precision=EXACT, preferred_element_type=F32)


def factorize(gram_ref, fac_ref, inv_ref):
    size = gram_ref.shape[0]
    fac_ref[...] = jnp.zeros_like(fac_ref)
    inv_ref[...] = jnp.zeros_like(inv_ref)
    for start in range(0, size, LEAF):
        here = pl.ds(start, LEAF)
        upper, left = leaf_factor(gram_ref[here, here])
        inv = left.T
        fac_ref[here, here] = upper
        rest = size - start - LEAF
        if rest:
            after = pl.ds(start + LEAF, rest)
            panel = exact_dot(left, gram_ref[here, after])
            fac_ref[here, after] = panel
            gram_ref[after, after] = gram_ref[after, after] - exact_dot(panel, panel, ((0,), (0,)))
        if start:
            before = pl.ds(0, start)
            above = exact_dot(fac_ref[before, here], inv)
            inv_ref[before, here] = -exact_dot(inv_ref[before, before], above)
        inv_ref[here, here] = inv


def kernel(
    n_row, n_col, nodes,
    a_ref, basis_ref, scale_ref,
    emb_ref, fac_ref,
    probe, img, scl, srow, rs_out, rs_in, g_out, g_in, g_all, gram, inv, image,
    sc_send, sc_recv, ag_send, ag_recv, rs_send, rs_recv, ga_send, ga_recv, gb_send, gb_recv,
):
    my_row, my_col = lax.axis_index("row"), lax.axis_index("col")
    rows, width = basis_ref.shape
    row_peers = [lax.rem(my_row + d, n_row) for d in range(1, n_row)]
    col_peers = [lax.rem(my_col + d, n_col) for d in range(1, n_col)]
    tile = 128

    barrier = pltpu.get_barrier_semaphore()
    for r in row_peers:
        pl.semaphore_signal(barrier, inc=1, device_id=(r, my_col), device_id_type=MESH)
    for c in col_peers:
        pl.semaphore_signal(barrier, inc=1, device_id=(my_row, c), device_id_type=MESH)
    pl.semaphore_wait(barrier, n_row + n_col - 2)

    def remote(src, dst, send, recv, device):
        return pltpu.make_async_remote_copy(
            src_ref=src, dst_ref=dst, send_sem=send, recv_sem=recv,
            device_id=device, device_id_type=MESH,
        )

    def start_gather(buf, send, recv):
        for r in row_peers:
            remote(buf.at[my_row], buf.at[my_row], send.at[r], recv.at[my_row], (r, my_col)).start()

    def wait_gather(buf, send, recv):
        for r in row_peers:
            remote(buf.at[my_row], buf.at[r], send.at[r], recv.at[r], (r, my_col)).wait()

    def start_cols(src, dst, send, recv, own_src):
        for c in col_peers:
            s = src.at[my_col] if own_src else src.at[c]
            remote(s, dst.at[my_col], send.at[c], recv.at[my_col], (my_row, c)).start()

    def wait_cols(src, dst, send, recv, own_src):
        for c in col_peers:
            s = src.at[my_col] if own_src else src.at[c]
            remote(s, dst.at[c], send.at[c], recv.at[c], (my_row, c)).wait()

    def column_sum(src, par):
        total = src[par, 0].astype(F32)
        for c in range(1, n_col):
            total = total + src[par, c].astype(F32)
        return total

    def scale_of(part):
        block = scl[pl.ds(part * rows if isinstance(part, int) else pl.multiple_of(part * rows, rows), rows), :]
        return jnp.concatenate([block] * (width // 128), axis=1)

    def make_probe(par):
        for r in range(n_row):
            probe[pl.ds(r * rows, rows), :] = (img[par, r].astype(F32) * scale_of(r)).astype(BF16)

    img[1, my_row] = basis_ref[...]
    srow[my_row] = scale_ref[...]
    start_gather(srow, sc_send, sc_recv)
    start_gather(img.at[1], ag_send.at[1], ag_recv.at[1])
    wait_gather(srow, sc_send, sc_recv)
    for r in range(n_row):
        for part in range(rows // tile):
            line = jnp.broadcast_to(srow[r, part : part + 1, :], (tile, tile))
            scl[pl.ds(r * rows + part * tile, tile), :] = line.T
    wait_gather(img.at[1], ag_send.at[1], ag_recv.at[1])
    make_probe(1)

    def gram_start(par):
        whole = img[par, 0]
        total = lax.dot_general(whole, whole, (((0,), (0,)), ((), ())), preferred_element_type=F32)
        for r in range(1, n_row):
            whole = img[par, r]
            total = total + lax.dot_general(
                whole, whole, (((0,), (0,)), ((), ())), preferred_element_type=F32
            )
        total = (total / nodes).astype(BF16)
        piece = width // n_col
        for c in range(n_col):
            g_out[c] = total[c * piece : (c + 1) * piece, :]
        g_in[par, my_col] = g_out[my_col]
        start_cols(g_out, g_in.at[par], ga_send.at[par], ga_recv.at[par], False)

    def gram_middle(par):
        wait_cols(g_out, g_in.at[par], ga_send.at[par], ga_recv.at[par], False)
        g_all[par, my_col] = column_sum(g_in, par).astype(BF16)
        start_cols(g_all.at[par], g_all.at[par], gb_send.at[par], gb_recv.at[par], True)

    def gram_end(par):
        wait_cols(g_all.at[par], g_all.at[par], gb_send.at[par], gb_recv.at[par], True)
        piece = width // n_col
        for c in range(n_col):
            gram[pl.ds(c * piece, piece), :] = g_all[par, c].astype(F32)
        factorize(gram, fac_ref, inv)

    for step in range(ITERS):
        par, last = step % 2, (step + 1) % 2
        if step:
            gram_start(last)

        @pl.loop(0, n_col)
        def _(c):
            block = a_ref[pl.ds(pl.multiple_of(c * rows, rows), rows), :]
            rs_out[c] = jnp.dot(block, probe[...], preferred_element_type=F32).astype(BF16)

        if step:
            gram_middle(last)
        rs_in[par, my_col] = rs_out[my_col]
        start_cols(rs_out, rs_in.at[par], rs_send.at[par], rs_recv.at[par], False)
        if step:
            gram_end(last)
        wait_cols(rs_out, rs_in.at[par], rs_send.at[par], rs_recv.at[par], False)
        own = column_sum(rs_in, par) * scale_of(my_row)
        if step:
            own = exact_dot(own, inv[...])
        image[...] = own
        img[par, my_row] = own.astype(BF16)
        start_gather(img.at[par], ag_send.at[par], ag_recv.at[par])
        wait_gather(img.at[par], ag_send.at[par], ag_recv.at[par])
        if step < ITERS - 1:
            make_probe(par)

    par = (ITERS - 1) % 2
    gram_start(par)
    gram_middle(par)
    gram_end(par)
    emb_ref[...] = exact_dot(image[...], inv[...])


def body(n_row, n_col, basis, degree_scale, tile_data, tile_index, tile_count):
    rows, width = basis.shape
    block = n_row * rows
    dense = densify(tile_data[:, 0], tile_index[:, 0], tile_count[:, 0], block)
    scale = jnp.pad(degree_scale.reshape(-1, 128), ((0, 8 - rows // 128), (0, 0)))
    vmem = pl.BlockSpec(memory_space=pltpu.VMEM)
    dma = pltpu.SemaphoreType.DMA
    piece = width // n_col
    nodes = block * n_col
    return pl.pallas_call(
        functools.partial(kernel, n_row, n_col, nodes),
        out_shape=(
            jax.ShapeDtypeStruct((rows, width), F32),
            jax.ShapeDtypeStruct((width, width), F32),
        ),
        in_specs=[vmem] * 3,
        out_specs=(vmem, vmem),
        scratch_shapes=[
            pltpu.VMEM((block, width), BF16),
            pltpu.VMEM((2, n_row, rows, width), BF16),
            pltpu.VMEM((block, 128), F32),
            pltpu.VMEM((n_row, 8, 128), F32),
            pltpu.VMEM((n_col, rows, width), BF16),
            pltpu.VMEM((2, n_col, rows, width), BF16),
            pltpu.VMEM((n_col, piece, width), BF16),
            pltpu.VMEM((2, n_col, piece, width), BF16),
            pltpu.VMEM((2, n_col, piece, width), BF16),
            pltpu.VMEM((width, width), F32),
            pltpu.VMEM((width, width), F32),
            pltpu.VMEM((rows, width), F32),
            dma((n_row,)), dma((n_row,)), dma((2, n_row)), dma((2, n_row)),
            dma((2, n_col)), dma((2, n_col)), dma((2, n_col)), dma((2, n_col)),
            dma((2, n_col)), dma((2, n_col)),
        ],
        compiler_params=pltpu.CompilerParams(
            collective_id=0, has_side_effects=True, vmem_limit_bytes=VMEM_BYTES
        ),
    )(dense, basis, scale)


def solution(mesh):
    placed = (
        P(("row", "col"), None),
        P(("row", "col")),
        P("row", "col", None, None, None),
        P("row", "col", None),
        P("row", "col"),
    )
    return jax.shard_map(
        functools.partial(body, mesh.shape["row"], mesh.shape["col"]),
        mesh=mesh,
        in_specs=placed,
        out_specs=(P(("row", "col"), None), P()),
        check_vma=False,
    )
```

```python
import functools

import jax
import jax.numpy as jnp
from jax import lax
from jax.experimental import pallas as pl
from jax.experimental.pallas import tpu as pltpu
from jax.sharding import PartitionSpec as P

ITERS = 4
LEAF = 128
STEP = 8
F32 = jnp.float32
BF16 = jnp.bfloat16
EXACT = lax.Precision.HIGHEST
MESH = pl.DeviceIdType.MESH
VMEM_BYTES = 56 * 1024 * 1024


def densify(tiles_ref, index_ref, count_ref, dense):
    trows, slots, tile, _ = tiles_ref.shape

    @pl.loop(0, trows)
    def _(t):
        here = pl.ds(pl.multiple_of(t * tile, tile), tile)
        for column in range(dense.shape[1] // tile):
            slot, live = jnp.int32(0), jnp.float32(0.0)
            for s in range(slots):
                hit = (index_ref[t, s] == column) & (s < count_ref[t, 0])
                slot = jnp.where(hit, s, slot)
                live = jnp.where(hit, 1.0, live)
            dense[here, pl.ds(column * tile, tile)] = (
                tiles_ref[t, slot].astype(F32) * live
            ).astype(BF16)


def leaf_factor(gram):
    size = gram.shape[0]
    rows = lax.broadcasted_iota(jnp.int32, (size, size), 0)
    lanes = lax.broadcasted_iota(jnp.int32, (size, size), 1)
    eye = (rows == lanes).astype(F32)

    sub = lax.broadcasted_iota(jnp.int32, (STEP, size), 0)

    def combine(factors, panel):
        total = factors[0] * panel[0:1, :]
        for k in range(1, STEP):
            total = total + factors[k] * panel[k : k + 1, :]
        return total

    def group(g, state):
        work, left = state
        cols = [jnp.broadcast_to(work[:, j : j + 1], (size, size)) for j in range(STEP)]
        block = [c[:STEP] for c in cols]
        lower = [(sub == j).astype(F32) for j in range(STEP)]
        full = list(lower)
        scale = jnp.ones((STEP, size), F32)
        for j in range(STEP):
            over = 1.0 / block[j][j : j + 1, :]
            ratio = jnp.where(sub == j, 0.0, block[j] * over)
            below = jnp.where(sub > j, ratio, 0.0)
            scale = jnp.where(sub == j, over, scale)
            for k in range(j + 1, STEP):
                block[k] = block[k] - ratio * block[k][j : j + 1, :]
            for k in range(j + 1):
                lower[k] = lower[k] - below * lower[k][j : j + 1, :]
                full[k] = full[k] - ratio * full[k][j : j + 1, :]
        full = [f * scale for f in full]
        work_panel, left_panel = work[:STEP], left[:STEP]
        open_rows = rows[STEP:] < size - STEP * g
        cols = [jnp.where(open_rows, c[STEP:], 0.0) for c in cols]
        work_rest = work[STEP:] - combine(cols, combine(full, work_panel))
        left_rest = left[STEP:] - combine(cols, combine(full, left_panel))
        work = jnp.concatenate([work_rest, combine(lower, work_panel)], axis=0)
        left = jnp.concatenate([left_rest, combine(lower, left_panel)], axis=0)
        work = pltpu.roll(work, size - STEP, 1)
        return work, left

    work, left = lax.fori_loop(0, size // STEP, group, (gram, eye))
    diagonal = jnp.sum(work * eye, axis=1, keepdims=True)
    inverse = lax.rsqrt(diagonal)
    upper = jnp.where(rows <= lanes, work * inverse, 0.0)
    return upper, left * inverse


def exact_dot(a, b, dims=((1,), (0,))):
    return lax.dot_general(a, b, (dims, ((), ())), precision=EXACT, preferred_element_type=F32)


def factorize(gram_ref, fac_ref, inv_ref):
    size = gram_ref.shape[0]
    fac_ref[...] = jnp.zeros_like(fac_ref)
    inv_ref[...] = jnp.zeros_like(inv_ref)
    for start in range(0, size, LEAF):
        here = pl.ds(start, LEAF)
        upper, left = leaf_factor(gram_ref[here, here])
        inv = left.T
        fac_ref[here, here] = upper
        rest = size - start - LEAF
        if rest:
            after = pl.ds(start + LEAF, rest)
            panel = exact_dot(left, gram_ref[here, after])
            fac_ref[here, after] = panel
            gram_ref[after, after] = gram_ref[after, after] - exact_dot(panel, panel, ((0,), (0,)))
        if start:
            before = pl.ds(0, start)
            above = exact_dot(fac_ref[before, here], inv)
            inv_ref[before, here] = -exact_dot(inv_ref[before, before], above)
        inv_ref[here, here] = inv


def kernel(
    n_row, n_col, nodes,
    tiles_ref, index_ref, count_ref, basis_ref, scale_ref,
    emb_ref, fac_ref,
    a_ref, probe, img, scl, srow, rs_out, rs_in, g_out, g_in, g_all, gram, inv, image,
    sc_send, sc_recv, ag_send, ag_recv, rs_send, rs_recv, ga_send, ga_recv, gb_send, gb_recv,
):
    my_row, my_col = lax.axis_index("row"), lax.axis_index("col")
    rows, width = basis_ref.shape
    row_peers = [lax.rem(my_row + d, n_row) for d in range(1, n_row)]
    col_peers = [lax.rem(my_col + d, n_col) for d in range(1, n_col)]
    tile = 128

    barrier = pltpu.get_barrier_semaphore()
    for r in row_peers:
        pl.semaphore_signal(barrier, inc=1, device_id=(r, my_col), device_id_type=MESH)
    for c in col_peers:
        pl.semaphore_signal(barrier, inc=1, device_id=(my_row, c), device_id_type=MESH)
    pl.semaphore_wait(barrier, n_row + n_col - 2)

    def remote(src, dst, send, recv, device):
        return pltpu.make_async_remote_copy(
            src_ref=src, dst_ref=dst, send_sem=send, recv_sem=recv,
            device_id=device, device_id_type=MESH,
        )

    def start_gather(buf, send, recv):
        for r in row_peers:
            remote(buf.at[my_row], buf.at[my_row], send.at[r], recv.at[my_row], (r, my_col)).start()

    def wait_gather(buf, send, recv):
        for r in row_peers:
            remote(buf.at[my_row], buf.at[r], send.at[r], recv.at[r], (r, my_col)).wait()

    def start_cols(src, dst, send, recv, own_src):
        for c in col_peers:
            s = src.at[my_col] if own_src else src.at[c]
            remote(s, dst.at[my_col], send.at[c], recv.at[my_col], (my_row, c)).start()

    def wait_cols(src, dst, send, recv, own_src):
        for c in col_peers:
            s = src.at[my_col] if own_src else src.at[c]
            remote(s, dst.at[c], send.at[c], recv.at[c], (my_row, c)).wait()

    def column_sum(src, par):
        total = src[par, 0].astype(F32)
        for c in range(1, n_col):
            total = total + src[par, c].astype(F32)
        return total

    def scale_of(part):
        block = scl[pl.ds(part * rows if isinstance(part, int) else pl.multiple_of(part * rows, rows), rows), :]
        return jnp.concatenate([block] * (width // 128), axis=1)

    def make_probe(par):
        for r in range(n_row):
            probe[pl.ds(r * rows, rows), :] = (img[par, r].astype(F32) * scale_of(r)).astype(BF16)

    img[1, my_row] = basis_ref[...]
    srow[my_row] = scale_ref[...]
    start_gather(srow, sc_send, sc_recv)
    start_gather(img.at[1], ag_send.at[1], ag_recv.at[1])
    densify(tiles_ref, index_ref, count_ref, a_ref)
    wait_gather(srow, sc_send, sc_recv)
    for r in range(n_row):
        for part in range(rows // tile):
            line = jnp.broadcast_to(srow[r, part : part + 1, :], (tile, tile))
            scl[pl.ds(r * rows + part * tile, tile), :] = line.T
    wait_gather(img.at[1], ag_send.at[1], ag_recv.at[1])
    make_probe(1)

    def gram_start(par):
        whole = img[par, 0]
        total = lax.dot_general(whole, whole, (((0,), (0,)), ((), ())), preferred_element_type=F32)
        for r in range(1, n_row):
            whole = img[par, r]
            total = total + lax.dot_general(
                whole, whole, (((0,), (0,)), ((), ())), preferred_element_type=F32
            )
        total = (total / nodes).astype(BF16)
        piece = width // n_col
        for c in range(n_col):
            g_out[c] = total[c * piece : (c + 1) * piece, :]
        g_in[par, my_col] = g_out[my_col]
        start_cols(g_out, g_in.at[par], ga_send.at[par], ga_recv.at[par], False)

    def gram_middle(par):
        wait_cols(g_out, g_in.at[par], ga_send.at[par], ga_recv.at[par], False)
        g_all[par, my_col] = column_sum(g_in, par).astype(BF16)
        start_cols(g_all.at[par], g_all.at[par], gb_send.at[par], gb_recv.at[par], True)

    def gram_end(par):
        wait_cols(g_all.at[par], g_all.at[par], gb_send.at[par], gb_recv.at[par], True)
        piece = width // n_col
        for c in range(n_col):
            gram[pl.ds(c * piece, piece), :] = g_all[par, c].astype(F32)
        factorize(gram, fac_ref, inv)

    for step in range(ITERS):
        par, last = step % 2, (step + 1) % 2
        if step:
            gram_start(last)

        @pl.loop(0, n_col)
        def _(c):
            block = a_ref[pl.ds(pl.multiple_of(c * rows, rows), rows), :]
            rs_out[c] = jnp.dot(block, probe[...], preferred_element_type=F32).astype(BF16)

        if step:
            gram_middle(last)
        rs_in[par, my_col] = rs_out[my_col]
        start_cols(rs_out, rs_in.at[par], rs_send.at[par], rs_recv.at[par], False)
        if step:
            gram_end(last)
        wait_cols(rs_out, rs_in.at[par], rs_send.at[par], rs_recv.at[par], False)
        own = column_sum(rs_in, par) * scale_of(my_row)
        if step:
            own = exact_dot(own, inv[...])
        image[...] = own
        img[par, my_row] = own.astype(BF16)
        start_gather(img.at[par], ag_send.at[par], ag_recv.at[par])
        wait_gather(img.at[par], ag_send.at[par], ag_recv.at[par])
        if step < ITERS - 1:
            make_probe(par)

    par = (ITERS - 1) % 2
    gram_start(par)
    gram_middle(par)
    gram_end(par)
    emb_ref[...] = exact_dot(image[...], inv[...])


def body(n_row, n_col, basis, degree_scale, tile_data, tile_index, tile_count):
    rows, width = basis.shape
    block = n_row * rows
    scale = jnp.pad(degree_scale.reshape(-1, 128), ((0, 8 - rows // 128), (0, 0)))
    vmem = pl.BlockSpec(memory_space=pltpu.VMEM)
    smem = pl.BlockSpec(memory_space=pltpu.SMEM)
    dma = pltpu.SemaphoreType.DMA
    piece = width // n_col
    nodes = block * n_col
    return pl.pallas_call(
        functools.partial(kernel, n_row, n_col, nodes),
        out_shape=(
            jax.ShapeDtypeStruct((rows, width), F32),
            jax.ShapeDtypeStruct((width, width), F32),
        ),
        in_specs=[vmem, smem, smem, vmem, vmem],
        out_specs=(vmem, vmem),
        scratch_shapes=[
            pltpu.VMEM((tile_data.shape[0] * tile_data.shape[-1], block), BF16),
            pltpu.VMEM((block, width), BF16),
            pltpu.VMEM((2, n_row, rows, width), BF16),
            pltpu.VMEM((block, 128), F32),
            pltpu.VMEM((n_row, 8, 128), F32),
            pltpu.VMEM((n_col, rows, width), BF16),
            pltpu.VMEM((2, n_col, rows, width), BF16),
            pltpu.VMEM((n_col, piece, width), BF16),
            pltpu.VMEM((2, n_col, piece, width), BF16),
            pltpu.VMEM((2, n_col, piece, width), BF16),
            pltpu.VMEM((width, width), F32),
            pltpu.VMEM((width, width), F32),
            pltpu.VMEM((rows, width), F32),
            dma((n_row,)), dma((n_row,)), dma((2, n_row)), dma((2, n_row)),
            dma((2, n_col)), dma((2, n_col)), dma((2, n_col)), dma((2, n_col)),
            dma((2, n_col)), dma((2, n_col)),
        ],
        compiler_params=pltpu.CompilerParams(
            collective_id=0, has_side_effects=True, vmem_limit_bytes=VMEM_BYTES
        ),
    )(tile_data[:, 0], tile_index[:, 0], tile_count, basis, scale)


def solution(mesh):
    placed = (
        P(("row", "col"), None),
        P(("row", "col")),
        P("row", "col", None, None, None),
        P("row", "col", None),
        P("row", "col"),
    )
    return jax.shard_map(
        functools.partial(body, mesh.shape["row"], mesh.shape["col"]),
        mesh=mesh,
        in_specs=placed,
        out_specs=(P(("row", "col"), None), P()),
        check_vma=False,
    )
```

```python
import functools

import jax
import jax.numpy as jnp
from jax import lax
from jax.experimental import pallas as pl
from jax.experimental.pallas import tpu as pltpu
from jax.sharding import PartitionSpec as P

ITERS = 4
LEAF = 128
DEEP = 4
STEP = 8
F32 = jnp.float32
BF16 = jnp.bfloat16
EXACT = lax.Precision.HIGHEST
MESH = pl.DeviceIdType.MESH
VMEM_BYTES = 56 * 1024 * 1024


def densify(tiles_ref, index_ref, count_ref, dense):
    trows, slots, tile, _ = tiles_ref.shape

    @pl.loop(0, trows)
    def _(t):
        here = pl.ds(pl.multiple_of(t * tile, tile), tile)
        for column in range(dense.shape[1] // tile):
            slot, live = jnp.int32(0), jnp.float32(0.0)
            for s in range(slots):
                hit = (index_ref[t, s] == column) & (s < count_ref[t, 0])
                slot = jnp.where(hit, s, slot)
                live = jnp.where(hit, 1.0, live)
            dense[here, pl.ds(column * tile, tile)] = (
                tiles_ref[t, slot].astype(F32) * live
            ).astype(BF16)


def leaf_factor(gram):
    size = gram.shape[0]
    rows = lax.broadcasted_iota(jnp.int32, (size, size), 0)
    lanes = lax.broadcasted_iota(jnp.int32, (size, size), 1)
    eye = (rows == lanes).astype(F32)

    sub = lax.broadcasted_iota(jnp.int32, (STEP, size), 0)

    def combine(factors, panel):
        total = factors[0] * panel[0:1, :]
        for k in range(1, STEP):
            total = total + factors[k] * panel[k : k + 1, :]
        return total

    def group(g, state):
        work, left = state
        cols = [jnp.broadcast_to(work[:, j : j + 1], (size, size)) for j in range(STEP)]
        block = [c[:STEP] for c in cols]
        lower = [(sub == j).astype(F32) for j in range(STEP)]
        full = list(lower)
        scale = jnp.ones((STEP, size), F32)
        for j in range(STEP):
            over = 1.0 / block[j][j : j + 1, :]
            ratio = jnp.where(sub == j, 0.0, block[j] * over)
            below = jnp.where(sub > j, ratio, 0.0)
            scale = jnp.where(sub == j, over, scale)
            for k in range(j + 1, STEP):
                block[k] = block[k] - ratio * block[k][j : j + 1, :]
            for k in range(j + 1):
                lower[k] = lower[k] - below * lower[k][j : j + 1, :]
                full[k] = full[k] - ratio * full[k][j : j + 1, :]
        full = [f * scale for f in full]
        work_panel, left_panel = work[:STEP], left[:STEP]
        open_rows = rows[STEP:] < size - STEP * g
        cols = [jnp.where(open_rows, c[STEP:], 0.0) for c in cols]
        work_rest = work[STEP:] - combine(cols, combine(full, work_panel))
        left_rest = left[STEP:] - combine(cols, combine(full, left_panel))
        work = jnp.concatenate([work_rest, combine(lower, work_panel)], axis=0)
        left = jnp.concatenate([left_rest, combine(lower, left_panel)], axis=0)
        work = pltpu.roll(work, size - STEP, 1)
        return work, left

    work, left = lax.fori_loop(0, size // STEP, group, (gram, eye))
    diagonal = jnp.sum(work * eye, axis=1, keepdims=True)
    inverse = lax.rsqrt(diagonal)
    upper = jnp.where(rows <= lanes, work * inverse, 0.0)
    return upper, left * inverse


def exact_dot(a, b, dims=((1,), (0,))):
    return lax.dot_general(a, b, (dims, ((), ())), precision=EXACT, preferred_element_type=F32)


def factorize(gram_ref, fac_ref, inv_ref, starts):
    size = gram_ref.shape[0]
    for start in starts:
        if not start:
            fac_ref[...] = jnp.zeros_like(fac_ref)
            inv_ref[...] = jnp.zeros_like(inv_ref)
        here = pl.ds(start, LEAF)
        upper, left = leaf_factor(gram_ref[here, here])
        inv = left.T
        fac_ref[here, here] = upper
        rest = size - start - LEAF
        if rest:
            after = pl.ds(start + LEAF, rest)
            panel = exact_dot(left, gram_ref[here, after])
            fac_ref[here, after] = panel
            gram_ref[after, after] = gram_ref[after, after] - exact_dot(panel, panel, ((0,), (0,)))
        if start:
            before = pl.ds(0, start)
            above = exact_dot(fac_ref[before, here], inv)
            inv_ref[before, here] = -exact_dot(inv_ref[before, before], above)
        inv_ref[here, here] = inv


def kernel(
    n_row, n_col, nodes,
    tiles_ref, index_ref, count_ref, basis_ref, scale_ref,
    emb_ref, fac_ref,
    a_ref, probe, img, scl, srow, rs_out, rs_in, g_out, g_in, g_all, gram, inv, image, s2_out, s2_in,
    sc_send, sc_recv, ag_send, ag_recv, rs_send, rs_recv, ga_send, ga_recv, gb_send, gb_recv, s2_send, s2_recv,
):
    my_row, my_col = lax.axis_index("row"), lax.axis_index("col")
    rows, width = basis_ref.shape
    row_peers = [lax.rem(my_row + d, n_row) for d in range(1, n_row)]
    col_peers = [lax.rem(my_col + d, n_col) for d in range(1, n_col)]
    tile = 128
    deep = min(DEEP, n_col)
    wide = n_col // deep
    my_z, my_y = my_col // wide, lax.rem(my_col, wide)
    starts = list(range(0, width, LEAF))

    barrier = pltpu.get_barrier_semaphore()
    for r in row_peers:
        pl.semaphore_signal(barrier, inc=1, device_id=(r, my_col), device_id_type=MESH)
    for c in col_peers:
        pl.semaphore_signal(barrier, inc=1, device_id=(my_row, c), device_id_type=MESH)
    pl.semaphore_wait(barrier, n_row + n_col - 2)

    def remote(src, dst, send, recv, device):
        return pltpu.make_async_remote_copy(
            src_ref=src, dst_ref=dst, send_sem=send, recv_sem=recv,
            device_id=device, device_id_type=MESH,
        )

    def start_gather(buf, send, recv):
        for r in row_peers:
            remote(buf.at[my_row], buf.at[my_row], send.at[r], recv.at[my_row], (r, my_col)).start()

    def wait_gather(buf, send, recv):
        for r in row_peers:
            remote(buf.at[my_row], buf.at[r], send.at[r], recv.at[r], (r, my_col)).wait()

    def start_cols(src, dst, send, recv, own_src):
        for c in col_peers:
            s = src.at[my_col] if own_src else src.at[c]
            remote(s, dst.at[my_col], send.at[c], recv.at[my_col], (my_row, c)).start()

    def wait_cols(src, dst, send, recv, own_src):
        for c in col_peers:
            s = src.at[my_col] if own_src else src.at[c]
            remote(s, dst.at[c], send.at[c], recv.at[c], (my_row, c)).wait()

    def column_sum(src, par):
        total = src[par, 0].astype(F32)
        for c in range(1, n_col):
            total = total + src[par, c].astype(F32)
        return total

    def scale_of(part):
        block = scl[pl.ds(part * rows if isinstance(part, int) else pl.multiple_of(part * rows, rows), rows), :]
        return jnp.concatenate([block] * (width // 128), axis=1)

    def make_probe(par):
        for r in range(n_row):
            probe[pl.ds(r * rows, rows), :] = (img[par, r].astype(F32) * scale_of(r)).astype(BF16)

    img[1, my_row] = basis_ref[...]
    srow[my_row] = scale_ref[...]
    start_gather(srow, sc_send, sc_recv)
    start_gather(img.at[1], ag_send.at[1], ag_recv.at[1])
    densify(tiles_ref, index_ref, count_ref, a_ref)
    wait_gather(srow, sc_send, sc_recv)
    for r in range(n_row):
        for part in range(rows // tile):
            line = jnp.broadcast_to(srow[r, part : part + 1, :], (tile, tile))
            scl[pl.ds(r * rows + part * tile, tile), :] = line.T
    wait_gather(img.at[1], ag_send.at[1], ag_recv.at[1])
    make_probe(1)

    def gram_start(par):
        whole = img[par, 0]
        total = lax.dot_general(whole, whole, (((0,), (0,)), ((), ())), preferred_element_type=F32)
        for r in range(1, n_row):
            whole = img[par, r]
            total = total + lax.dot_general(
                whole, whole, (((0,), (0,)), ((), ())), preferred_element_type=F32
            )
        total = (total / nodes).astype(BF16)
        piece = width // n_col
        for c in range(n_col):
            g_out[c] = total[c * piece : (c + 1) * piece, :]
        g_in[par, my_col] = g_out[my_col]
        start_cols(g_out, g_in.at[par], ga_send.at[par], ga_recv.at[par], False)

    def gram_middle(par):
        wait_cols(g_out, g_in.at[par], ga_send.at[par], ga_recv.at[par], False)
        g_all[par, my_col] = column_sum(g_in, par).astype(BF16)
        start_cols(g_all.at[par], g_all.at[par], gb_send.at[par], gb_recv.at[par], True)

    def gram_end(par):
        wait_cols(g_all.at[par], g_all.at[par], gb_send.at[par], gb_recv.at[par], True)
        piece = width // n_col
        for c in range(n_col):
            gram[pl.ds(c * piece, piece), :] = g_all[par, c].astype(F32)
        factorize(gram, fac_ref, inv, starts[:1])

    def first_stage(par, d, begin):
        z = lax.rem(my_z + d, deep)
        for e in range(1, wide):
            y = lax.rem(my_y + e, wide)
            chunk = z * wide + y
            slot = my_y * deep + z if begin else y * deep + z
            copy = remote(
                rs_out.at[chunk], rs_in.at[par, slot],
                rs_send.at[par, chunk], rs_recv.at[par, slot], (my_row, my_z * wide + y),
            )
            copy.start() if begin else copy.wait()

    def first_sum(par, d):
        z = lax.rem(my_z + d, deep)
        total = rs_out[z * wide + my_y].astype(F32)
        for e in range(1, wide):
            y = lax.rem(my_y + e, wide)
            total = total + rs_in[par, y * deep + z].astype(F32)
        return total

    def second_stage(par, d, begin):
        z = lax.rem(my_z + d, deep)
        slot = my_z if begin else z
        copy = remote(
            s2_out.at[z], s2_in.at[par, slot],
            s2_send.at[par, z], s2_recv.at[par, slot], (my_row, z * wide + my_y),
        )
        copy.start() if begin else copy.wait()

    for step in range(ITERS):
        par, last = step % 2, (step + 1) % 2
        if step:
            gram_start(last)

        @pl.loop(0, n_col)
        def _(c):
            block = a_ref[pl.ds(pl.multiple_of(c * rows, rows), rows), :]
            rs_out[c] = jnp.dot(block, probe[...], preferred_element_type=F32).astype(BF16)

        if step:
            gram_middle(last)
        depths = list(range(1, deep))
        for d in depths + [0]:
            first_stage(par, d, True)
        if step:
            gram_end(last)
        for d in depths:
            first_stage(par, d, False)
            s2_out[lax.rem(my_z + d, deep)] = first_sum(par, d).astype(BF16)
            second_stage(par, d, True)
        if step:
            factorize(gram, fac_ref, inv, starts[1:])
        first_stage(par, 0, False)
        own = first_sum(par, 0)
        for d in depths:
            second_stage(par, d, False)
            own = own + s2_in[par, lax.rem(my_z + d, deep)].astype(F32)
        own = own * scale_of(my_row)
        if step:
            own = exact_dot(own, inv[...])
        image[...] = own
        img[par, my_row] = own.astype(BF16)
        start_gather(img.at[par], ag_send.at[par], ag_recv.at[par])
        wait_gather(img.at[par], ag_send.at[par], ag_recv.at[par])
        if step < ITERS - 1:
            make_probe(par)

    par = (ITERS - 1) % 2
    gram_start(par)
    gram_middle(par)
    gram_end(par)
    factorize(gram, fac_ref, inv, starts[1:])
    emb_ref[...] = exact_dot(image[...], inv[...])


def body(n_row, n_col, basis, degree_scale, tile_data, tile_index, tile_count):
    rows, width = basis.shape
    block = n_row * rows
    scale = jnp.pad(degree_scale.reshape(-1, 128), ((0, 8 - rows // 128), (0, 0)))
    vmem = pl.BlockSpec(memory_space=pltpu.VMEM)
    smem = pl.BlockSpec(memory_space=pltpu.SMEM)
    dma = pltpu.SemaphoreType.DMA
    piece = width // n_col
    nodes = block * n_col
    return pl.pallas_call(
        functools.partial(kernel, n_row, n_col, nodes),
        out_shape=(
            jax.ShapeDtypeStruct((rows, width), F32),
            jax.ShapeDtypeStruct((width, width), F32),
        ),
        in_specs=[vmem, smem, smem, vmem, vmem],
        out_specs=(vmem, vmem),
        scratch_shapes=[
            pltpu.VMEM((tile_data.shape[0] * tile_data.shape[-1], block), BF16),
            pltpu.VMEM((block, width), BF16),
            pltpu.VMEM((2, n_row, rows, width), BF16),
            pltpu.VMEM((block, 128), F32),
            pltpu.VMEM((n_row, 8, 128), F32),
            pltpu.VMEM((n_col, rows, width), BF16),
            pltpu.VMEM((2, n_col, rows, width), BF16),
            pltpu.VMEM((n_col, piece, width), BF16),
            pltpu.VMEM((2, n_col, piece, width), BF16),
            pltpu.VMEM((2, n_col, piece, width), BF16),
            pltpu.VMEM((width, width), F32),
            pltpu.VMEM((width, width), F32),
            pltpu.VMEM((rows, width), F32),
            pltpu.VMEM((min(DEEP, n_col), rows, width), BF16),
            pltpu.VMEM((2, min(DEEP, n_col), rows, width), BF16),
            dma((n_row,)), dma((n_row,)), dma((2, n_row)), dma((2, n_row)),
            dma((2, n_col)), dma((2, n_col)), dma((2, n_col)), dma((2, n_col)),
            dma((2, n_col)), dma((2, n_col)), dma((2, min(DEEP, n_col))), dma((2, min(DEEP, n_col))),
        ],
        compiler_params=pltpu.CompilerParams(
            collective_id=0, has_side_effects=True, vmem_limit_bytes=VMEM_BYTES
        ),
    )(tile_data[:, 0], tile_index[:, 0], tile_count, basis, scale)


def solution(mesh):
    placed = (
        P(("row", "col"), None),
        P(("row", "col")),
        P("row", "col", None, None, None),
        P("row", "col", None),
        P("row", "col"),
    )
    return jax.shard_map(
        functools.partial(body, mesh.shape["row"], mesh.shape["col"]),
        mesh=mesh,
        in_specs=placed,
        out_specs=(P(("row", "col"), None), P()),
        check_vma=False,
    )
```

```python
import functools

import jax
import jax.numpy as jnp
from jax import lax
from jax.experimental import pallas as pl
from jax.experimental.pallas import tpu as pltpu
from jax.sharding import PartitionSpec as P

ITERS = 4
LEAF = 128
DEEP = 4
STEP = 8
F32 = jnp.float32
BF16 = jnp.bfloat16
EXACT = lax.Precision.HIGHEST
MESH = pl.DeviceIdType.MESH
VMEM_BYTES = 56 * 1024 * 1024


def densify(tiles_ref, index_ref, count_ref, dense):
    trows, slots, tile, _ = tiles_ref.shape

    @pl.loop(0, trows)
    def _(t):
        here = pl.ds(pl.multiple_of(t * tile, tile), tile)
        for column in range(dense.shape[1] // tile):
            slot, live = jnp.int32(0), jnp.float32(0.0)
            for s in range(slots):
                hit = (index_ref[t, s] == column) & (s < count_ref[t, 0])
                slot = jnp.where(hit, s, slot)
                live = jnp.where(hit, 1.0, live)
            dense[here, pl.ds(column * tile, tile)] = (
                tiles_ref[t, slot].astype(F32) * live
            ).astype(BF16)


def leaf_factor(gram):
    size = gram.shape[0]
    rows = lax.broadcasted_iota(jnp.int32, (size, size), 0)
    lanes = lax.broadcasted_iota(jnp.int32, (size, size), 1)
    eye = (rows == lanes).astype(F32)

    sub = lax.broadcasted_iota(jnp.int32, (STEP, size), 0)

    def combine(factors, panel):
        total = factors[0] * panel[0:1, :]
        for k in range(1, STEP):
            total = total + factors[k] * panel[k : k + 1, :]
        return total

    def group(g, state):
        work, left = state
        cols = [jnp.broadcast_to(work[:, j : j + 1], (size, size)) for j in range(STEP)]
        block = [c[:STEP] for c in cols]
        lower = [(sub == j).astype(F32) for j in range(STEP)]
        full = list(lower)
        scale = jnp.ones((STEP, size), F32)
        for j in range(STEP):
            over = 1.0 / block[j][j : j + 1, :]
            ratio = jnp.where(sub == j, 0.0, block[j] * over)
            below = jnp.where(sub > j, ratio, 0.0)
            scale = jnp.where(sub == j, over, scale)
            for k in range(j + 1, STEP):
                block[k] = block[k] - ratio * block[k][j : j + 1, :]
            for k in range(j + 1):
                lower[k] = lower[k] - below * lower[k][j : j + 1, :]
                full[k] = full[k] - ratio * full[k][j : j + 1, :]
        full = [f * scale for f in full]
        work_panel, left_panel = work[:STEP], left[:STEP]
        open_rows = rows[STEP:] < size - STEP * g
        cols = [jnp.where(open_rows, c[STEP:], 0.0) for c in cols]
        work_rest = work[STEP:] - combine(cols, combine(full, work_panel))
        left_rest = left[STEP:] - combine(cols, combine(full, left_panel))
        work = jnp.concatenate([work_rest, combine(lower, work_panel)], axis=0)
        left = jnp.concatenate([left_rest, combine(lower, left_panel)], axis=0)
        work = pltpu.roll(work, size - STEP, 1)
        return work, left

    work, left = lax.fori_loop(0, size // STEP, group, (gram, eye))
    diagonal = jnp.sum(work * eye, axis=1, keepdims=True)
    inverse = lax.rsqrt(diagonal)
    upper = jnp.where(rows <= lanes, work * inverse, 0.0)
    return upper, left * inverse


def exact_dot(a, b, dims=((1,), (0,))):
    return lax.dot_general(a, b, (dims, ((), ())), precision=EXACT, preferred_element_type=F32)


def factorize(gram_ref, fac_ref, inv_ref, starts):
    size = gram_ref.shape[0]
    for start in starts:
        if not start:
            fac_ref[...] = jnp.zeros_like(fac_ref)
            inv_ref[...] = jnp.zeros_like(inv_ref)
        here = pl.ds(start, LEAF)
        upper, left = leaf_factor(gram_ref[here, here])
        inv = left.T
        fac_ref[here, here] = upper
        rest = size - start - LEAF
        if rest:
            after = pl.ds(start + LEAF, rest)
            panel = exact_dot(left, gram_ref[here, after])
            fac_ref[here, after] = panel
            gram_ref[after, after] = gram_ref[after, after] - exact_dot(panel, panel, ((0,), (0,)))
        if start:
            before = pl.ds(0, start)
            above = exact_dot(fac_ref[before, here], inv)
            inv_ref[before, here] = -exact_dot(inv_ref[before, before], above)
        inv_ref[here, here] = inv


def kernel(
    n_row, n_col, nodes,
    tiles_ref, index_ref, count_ref, basis_ref, scale_ref,
    emb_ref, fac_ref,
    a_ref, probe, img, scl, srow, rs_out, rs_in, g_out, g_in, g_all, gram, inv, image, s2_out, s2_in,
    sc_send, sc_recv, ag_send, ag_recv, rs_send, rs_recv, ga_send, ga_recv, gb_send, gb_recv, s2_send, s2_recv,
):
    my_row, my_col = lax.axis_index("row"), lax.axis_index("col")
    rows, width = basis_ref.shape
    row_peers = [lax.rem(my_row + d, n_row) for d in range(1, n_row)]
    col_peers = [lax.rem(my_col + d, n_col) for d in range(1, n_col)]
    tile = 128
    deep = min(DEEP, n_col)
    wide = n_col // deep
    my_z, my_y = my_col // wide, lax.rem(my_col, wide)
    starts = list(range(0, width, LEAF))

    barrier = pltpu.get_barrier_semaphore()
    for r in row_peers:
        pl.semaphore_signal(barrier, inc=1, device_id=(r, my_col), device_id_type=MESH)
    for c in col_peers:
        pl.semaphore_signal(barrier, inc=1, device_id=(my_row, c), device_id_type=MESH)
    pl.semaphore_wait(barrier, n_row + n_col - 2)

    def remote(src, dst, send, recv, device):
        return pltpu.make_async_remote_copy(
            src_ref=src, dst_ref=dst, send_sem=send, recv_sem=recv,
            device_id=device, device_id_type=MESH,
        )

    mate = my_row + 1 - 2 * lax.rem(my_row, 2)
    same = [lax.rem(my_row + 2 * d, n_row) for d in range(1, n_row // 2)]

    def start_gather(buf, send, recv):
        for r in same + [mate]:
            remote(buf.at[my_row], buf.at[my_row], send.at[r], recv.at[my_row], (r, my_col)).start()

    def wait_gather(buf, send, recv):
        across = [r + 1 - 2 * lax.rem(r, 2) for r in same]
        for r, a in zip(same, across):
            remote(buf.at[my_row], buf.at[r], send.at[r], recv.at[r], (r, my_col)).wait()
            remote(buf.at[r], buf.at[r], send.at[a], recv.at[r], (mate, my_col)).start()
        remote(buf.at[my_row], buf.at[mate], send.at[mate], recv.at[mate], (mate, my_col)).wait()
        for r, a in zip(same, across):
            remote(buf.at[r], buf.at[a], send.at[a], recv.at[a], (mate, my_col)).wait()

    def start_cols(src, dst, send, recv, own_src):
        for c in col_peers:
            s = src.at[my_col] if own_src else src.at[c]
            remote(s, dst.at[my_col], send.at[c], recv.at[my_col], (my_row, c)).start()

    def wait_cols(src, dst, send, recv, own_src):
        for c in col_peers:
            s = src.at[my_col] if own_src else src.at[c]
            remote(s, dst.at[c], send.at[c], recv.at[c], (my_row, c)).wait()

    def column_sum(src, par):
        total = src[par, 0].astype(F32)
        for c in range(1, n_col):
            total = total + src[par, c].astype(F32)
        return total

    def scale_of(part):
        block = scl[pl.ds(part * rows if isinstance(part, int) else pl.multiple_of(part * rows, rows), rows), :]
        return jnp.concatenate([block] * (width // 128), axis=1)

    def make_probe(par):
        for r in range(n_row):
            probe[pl.ds(r * rows, rows), :] = (img[par, r].astype(F32) * scale_of(r)).astype(BF16)

    img[1, my_row] = basis_ref[...]
    srow[my_row] = scale_ref[...]
    start_gather(srow, sc_send, sc_recv)
    start_gather(img.at[1], ag_send.at[1], ag_recv.at[1])
    densify(tiles_ref, index_ref, count_ref, a_ref)
    wait_gather(srow, sc_send, sc_recv)
    for r in range(n_row):
        for part in range(rows // tile):
            line = jnp.broadcast_to(srow[r, part : part + 1, :], (tile, tile))
            scl[pl.ds(r * rows + part * tile, tile), :] = line.T
    wait_gather(img.at[1], ag_send.at[1], ag_recv.at[1])
    make_probe(1)

    def gram_start(par):
        whole = img[par, 0]
        total = lax.dot_general(whole, whole, (((0,), (0,)), ((), ())), preferred_element_type=F32)
        for r in range(1, n_row):
            whole = img[par, r]
            total = total + lax.dot_general(
                whole, whole, (((0,), (0,)), ((), ())), preferred_element_type=F32
            )
        total = (total / nodes).astype(BF16)
        piece = width // n_col
        for c in range(n_col):
            g_out[c] = total[c * piece : (c + 1) * piece, :]
        g_in[par, my_col] = g_out[my_col]
        start_cols(g_out, g_in.at[par], ga_send.at[par], ga_recv.at[par], False)

    def gram_middle(par):
        wait_cols(g_out, g_in.at[par], ga_send.at[par], ga_recv.at[par], False)
        g_all[par, my_col] = column_sum(g_in, par).astype(BF16)
        start_cols(g_all.at[par], g_all.at[par], gb_send.at[par], gb_recv.at[par], True)

    def gram_end(par):
        wait_cols(g_all.at[par], g_all.at[par], gb_send.at[par], gb_recv.at[par], True)
        piece = width // n_col
        for c in range(n_col):
            gram[pl.ds(c * piece, piece), :] = g_all[par, c].astype(F32)
        factorize(gram, fac_ref, inv, starts[:1])

    def first_stage(par, d, begin):
        z = lax.rem(my_z + d, deep)
        for e in range(1, wide):
            y = lax.rem(my_y + e, wide)
            chunk = z * wide + y
            slot = my_y * deep + z if begin else y * deep + z
            copy = remote(
                rs_out.at[chunk], rs_in.at[par, slot],
                rs_send.at[par, chunk], rs_recv.at[par, slot], (my_row, my_z * wide + y),
            )
            copy.start() if begin else copy.wait()

    def first_sum(par, d):
        z = lax.rem(my_z + d, deep)
        total = rs_out[z * wide + my_y].astype(F32)
        for e in range(1, wide):
            y = lax.rem(my_y + e, wide)
            total = total + rs_in[par, y * deep + z].astype(F32)
        return total

    def second_stage(par, d, begin):
        z = lax.rem(my_z + d, deep)
        slot = my_z if begin else z
        copy = remote(
            s2_out.at[z], s2_in.at[par, slot],
            s2_send.at[par, z], s2_recv.at[par, slot], (my_row, z * wide + my_y),
        )
        copy.start() if begin else copy.wait()

    for step in range(ITERS):
        par, last = step % 2, (step + 1) % 2
        if step:
            gram_start(last)

        @pl.loop(0, n_col)
        def _(c):
            block = a_ref[pl.ds(pl.multiple_of(c * rows, rows), rows), :]
            rs_out[c] = jnp.dot(block, probe[...], preferred_element_type=F32).astype(BF16)

        if step:
            gram_middle(last)
        depths = list(range(1, deep))
        for d in depths + [0]:
            first_stage(par, d, True)
        if step:
            gram_end(last)
        for d in depths:
            first_stage(par, d, False)
            s2_out[lax.rem(my_z + d, deep)] = first_sum(par, d).astype(BF16)
            second_stage(par, d, True)
        if step:
            factorize(gram, fac_ref, inv, starts[1:])
        first_stage(par, 0, False)
        own = first_sum(par, 0)
        for d in depths:
            second_stage(par, d, False)
            own = own + s2_in[par, lax.rem(my_z + d, deep)].astype(F32)
        own = own * scale_of(my_row)
        if step:
            own = exact_dot(own, inv[...])
        image[...] = own
        img[par, my_row] = own.astype(BF16)
        start_gather(img.at[par], ag_send.at[par], ag_recv.at[par])
        wait_gather(img.at[par], ag_send.at[par], ag_recv.at[par])
        if step < ITERS - 1:
            make_probe(par)

    par = (ITERS - 1) % 2
    gram_start(par)
    gram_middle(par)
    gram_end(par)
    factorize(gram, fac_ref, inv, starts[1:])
    emb_ref[...] = exact_dot(image[...], inv[...])


def body(n_row, n_col, basis, degree_scale, tile_data, tile_index, tile_count):
    rows, width = basis.shape
    block = n_row * rows
    scale = jnp.pad(degree_scale.reshape(-1, 128), ((0, 8 - rows // 128), (0, 0)))
    vmem = pl.BlockSpec(memory_space=pltpu.VMEM)
    smem = pl.BlockSpec(memory_space=pltpu.SMEM)
    dma = pltpu.SemaphoreType.DMA
    piece = width // n_col
    nodes = block * n_col
    return pl.pallas_call(
        functools.partial(kernel, n_row, n_col, nodes),
        out_shape=(
            jax.ShapeDtypeStruct((rows, width), F32),
            jax.ShapeDtypeStruct((width, width), F32),
        ),
        in_specs=[vmem, smem, smem, vmem, vmem],
        out_specs=(vmem, vmem),
        scratch_shapes=[
            pltpu.VMEM((tile_data.shape[0] * tile_data.shape[-1], block), BF16),
            pltpu.VMEM((block, width), BF16),
            pltpu.VMEM((2, n_row, rows, width), BF16),
            pltpu.VMEM((block, 128), F32),
            pltpu.VMEM((n_row, 8, 128), F32),
            pltpu.VMEM((n_col, rows, width), BF16),
            pltpu.VMEM((2, n_col, rows, width), BF16),
            pltpu.VMEM((n_col, piece, width), BF16),
            pltpu.VMEM((2, n_col, piece, width), BF16),
            pltpu.VMEM((2, n_col, piece, width), BF16),
            pltpu.VMEM((width, width), F32),
            pltpu.VMEM((width, width), F32),
            pltpu.VMEM((rows, width), F32),
            pltpu.VMEM((min(DEEP, n_col), rows, width), BF16),
            pltpu.VMEM((2, min(DEEP, n_col), rows, width), BF16),
            dma((n_row,)), dma((n_row,)), dma((2, n_row)), dma((2, n_row)),
            dma((2, n_col)), dma((2, n_col)), dma((2, n_col)), dma((2, n_col)),
            dma((2, n_col)), dma((2, n_col)), dma((2, min(DEEP, n_col))), dma((2, min(DEEP, n_col))),
        ],
        compiler_params=pltpu.CompilerParams(
            collective_id=0, has_side_effects=True, vmem_limit_bytes=VMEM_BYTES
        ),
    )(tile_data[:, 0], tile_index[:, 0], tile_count, basis, scale)


def solution(mesh):
    placed = (
        P(("row", "col"), None),
        P(("row", "col")),
        P("row", "col", None, None, None),
        P("row", "col", None),
        P("row", "col"),
    )
    return jax.shard_map(
        functools.partial(body, mesh.shape["row"], mesh.shape["col"]),
        mesh=mesh,
        in_specs=placed,
        out_specs=(P(("row", "col"), None), P()),
        check_vma=False,
    )
```
